32 devices in a mesh: sec: 2 (over core), tile: 16 (over z, y, x).
Axes of the slice: x: 2, y: 2, z: 4, core: 2. Of those that a mesh axis runs over, the one named last changes fastest.
Arguments:
- object_field: bfloat16 [2, 2, 4096, 512], P(None, 'sec', 'tile'), may hold values from -1 to 1
- probe: bfloat16 [2, 256, 256], replicated, may hold values from -6 to 6
- phases: float32 [256], replicated, may hold values from -3.140625 to 3.140625
- intensities: bfloat16 [32, 256, 256], P('tile'), may hold values from 0.099609375 to 2
- pos_row: int32 [32], P('tile'), may hold values from 0 to 255
- pos_col: int32 [32], P('tile'), may hold values from 0 to 256
- counts: int32 [16], P('tile'), may hold values from 1 to 2, as said below
Outputs:
- object_gradient: float32 [2, 2, 4096, 512], P(None, 'sec', 'tile')
The draws below stay inside these ranges and needn't reach their ends.
Inputs may be any that keep to these rules, and one draw needn't show every extreme that they name: `counts`: every strip has at least one live position, and some strip has exactly 2 in every draw.
All inputs are finite; a program needn't handle non-finite values.
Results may differ from the reference program's by a relative error of at most 0.025.
Values may be sent and summed in bfloat16 or wider, within the bound.
No kernel may reach another device: no remote copies, remote signals or barrier semaphores. Data moves between devices by JAX's collectives and lax.ppermute only.
A program may use at most 64 MiB of HBM per device.

```python
import math
import jax
import jax.numpy as jnp
from jax import lax

WAVE = 256
P_DEV = 2
COLS = 512
SLICES = 2
TILES = 16
NX = 4096
POS = 32


def draw_counts(key, part):
    base_count = jax.random.randint(jax.random.fold_in(key, 1), (TILES,), 1, max(P_DEV // 2, 1) + 1)
    full_tile = jax.random.randint(jax.random.fold_in(key, 2), (TILES,), 0, 8) == 0
    chosen = jax.random.randint(jax.random.fold_in(key, 3), (), 0, TILES)
    position_ids = jnp.arange(TILES, dtype=jnp.int32)
    return jnp.where(full_tile | (position_ids == chosen), P_DEV, base_count).astype(jnp.int32)


def plant(values, own_key, least, high):
    dims = values.shape
    index_at = [jax.random.randint(jax.random.fold_in(own_key, axis), (), 0, dims[axis]) for axis in range(len(dims))]
    values = values.at[tuple(index_at)].set(least)
    longest = dims.index(max(dims))
    index_at[longest] = (index_at[longest] + 1) % dims[longest]
    return values.at[tuple(index_at)].set(high)


def level_of(key, dims, shards, least, high):
    loudness, own = 1.0, jax.random.fold_in(key, 6)
    for axis_at, blocks in shards:
        steps = jnp.exp(jax.random.uniform(jax.random.fold_in(own, axis_at), (blocks,), jnp.float32, least / len(shards), high / len(shards)))
        loudness = loudness * jnp.repeat(steps, dims[axis_at] // blocks).reshape([-1 if axis == axis_at else 1 for axis in range(len(dims))])
    return loudness


def normal_values(stream_key, dims, scale, bound, kind=jnp.bfloat16):
    array = scale * jax.random.normal(stream_key, dims, jnp.float32)
    return jnp.clip(array, min=-bound, max=bound).astype(kind)


def setup_inputs(seed: int = 0) -> dict:
    streams_of = jax.random.split(jax.random.key(seed), 8)
    object_field = jnp.clip(jax.random.uniform(streams_of[0], (2, SLICES, NX, COLS), jnp.float32, -1.0, 1.0) * level_of(streams_of[0], (2, SLICES, NX, COLS), ((1, 2), (2, 16)), -0.4, 0.0), -1.0, 1.0).astype(jnp.bfloat16)
    probe = normal_values(streams_of[1], (2, WAVE, WAVE), 1.0, 6.0)
    phases = jnp.clip(jax.random.uniform(streams_of[2], (WAVE,), jnp.float32, -3.140625, 3.140625), -3.140625, 3.140625)
    intensities = jnp.clip(jnp.exp(math.log(2.0) - 2.9996462 * jax.random.uniform(streams_of[3], (POS, WAVE, WAVE), jnp.float32) ** level_of(streams_of[3], (POS, WAVE, WAVE), ((0, 16),), -0.2, 0.2)), 0.099609375, 2.0).astype(jnp.bfloat16)
    pos_row = plant(jax.random.randint(streams_of[4], (POS,), 0, WAVE), jax.random.fold_in(streams_of[4], 1), 0, WAVE - 1).astype(jnp.int32)
    pos_col = plant(jax.random.randint(streams_of[5], (POS,), 0, COLS - WAVE + 1), jax.random.fold_in(streams_of[5], 1), 0, COLS - WAVE).astype(jnp.int32)
    counts = draw_counts(jax.random.fold_in(streams_of[7], 71), 0)
    return dict(object_field=object_field, probe=probe, phases=phases, intensities=intensities, pos_row=pos_row, pos_col=pos_col, counts=counts)


def build_tables(phases, wave_side):
    frequency = jnp.arange(wave_side, dtype=jnp.int32)
    product = frequency[:, None] * frequency[None, :] % wave_side
    angles = product.astype(jnp.float32) * (2.0 * math.pi / wave_side)
    cosine = jnp.cos(angles)
    sine_table = jnp.sin(angles)
    turned = phases[:, None] + angles
    turned_re = jnp.cos(turned)
    turned_im = jnp.sin(turned)
    highest = lax.Precision.HIGHEST
    kernel_re = (jnp.dot(turned_re.T, cosine, precision=highest, preferred_element_type=jnp.float32) + jnp.dot(turned_im.T, sine_table, precision=highest, preferred_element_type=jnp.float32)) / wave_side
    kernel_im = (jnp.dot(turned_im.T, cosine, precision=highest, preferred_element_type=jnp.float32) - jnp.dot(turned_re.T, sine_table, precision=highest, preferred_element_type=jnp.float32)) / wave_side
    norm_scale = 1.0 / math.sqrt(wave_side)
    far_re = cosine * norm_scale
    far_im = -sine_table * norm_scale
    return (kernel_re.astype(jnp.bfloat16), kernel_im.astype(jnp.bfloat16), far_re.astype(jnp.bfloat16), far_im.astype(jnp.bfloat16))

def left_product(matrix, field):
    return jnp.einsum('mj,bjn->bmn', matrix.astype(jnp.float32), field.astype(jnp.float32), precision=lax.Precision.HIGHEST)

def right_product(field, matrix):
    return jnp.einsum('bmj,nj->bmn', field.astype(jnp.float32), matrix.astype(jnp.float32), precision=lax.Precision.HIGHEST)

def propagate(matrix_re, matrix_im, field_re, field_im):
    inner_re = (left_product(matrix_re, field_re) - left_product(matrix_im, field_im)).astype(jnp.bfloat16)
    inner_im = (left_product(matrix_re, field_im) + left_product(matrix_im, field_re)).astype(jnp.bfloat16)
    outer_re = (right_product(inner_re, matrix_re) - right_product(inner_im, matrix_im)).astype(jnp.bfloat16)
    outer_im = (right_product(inner_re, matrix_im) + right_product(inner_im, matrix_re)).astype(jnp.bfloat16)
    return (outer_re, outer_im)

def transmit(trans_re, trans_im, wave_re, wave_im):
    t_re = trans_re.astype(jnp.float32)
    t_im = trans_im.astype(jnp.float32)
    w_re = wave_re.astype(jnp.float32)
    w_im = wave_im.astype(jnp.float32)
    return ((t_re * w_re - t_im * w_im).astype(jnp.bfloat16), (t_re * w_im + t_im * w_re).astype(jnp.bfloat16))

def conj_times(first_re, first_im, second_re, second_im):
    a_re = first_re.astype(jnp.float32)
    a_im = first_im.astype(jnp.float32)
    b_re = second_re.astype(jnp.float32)
    b_im = second_im.astype(jnp.float32)
    return (a_re * b_re + a_im * b_im, a_re * b_im - a_im * b_re)

def reference(object_field, probe, phases, intensities, pos_row, pos_col, counts):
    kernel_re, kernel_im, far_re, far_im = build_tables(phases, WAVE)
    matrices = []
    for layer_index in range(SLICES):
        if layer_index == SLICES - 1:
            matrices.append((far_re, far_im))
        else:
            matrices.append((kernel_re, kernel_im))
    padded = jnp.concatenate([object_field, jnp.zeros((2, SLICES, WAVE, COLS), jnp.bfloat16)], axis=2)
    gradient = jnp.zeros((2, SLICES, NX + WAVE, COLS), jnp.float32)
    anchor = jnp.zeros((), jnp.int32)

    def per_tile(gradient, tile_index):
        first_slot = (tile_index * P_DEV).astype(jnp.int32)
        row_offsets = lax.dynamic_slice_in_dim(pos_row, first_slot, P_DEV)
        col_offsets = lax.dynamic_slice_in_dim(pos_col, first_slot, P_DEV)
        measured = lax.dynamic_slice_in_dim(intensities, first_slot, P_DEV, 0).astype(jnp.float32)
        weights = (jnp.arange(P_DEV, dtype=jnp.int32) < counts[tile_index]).astype(jnp.float32)
        starts = (tile_index * WAVE + row_offsets).astype(jnp.int32)

        def cut_window(top_row, left_col):
            return lax.dynamic_slice(padded, (anchor, anchor, top_row, left_col), (2, SLICES, WAVE, WAVE))
        windows = jax.vmap(cut_window)(starts, col_offsets)
        wave_re = jnp.broadcast_to(probe[0], (P_DEV, WAVE, WAVE))
        wave_im = jnp.broadcast_to(probe[1], (P_DEV, WAVE, WAVE))
        entries = []
        for layer_index in range(SLICES):
            entries.append((wave_re, wave_im))
            mixed_re, mixed_im = transmit(windows[:, 0, layer_index], windows[:, 1, layer_index], wave_re, wave_im)
            wave_re, wave_im = propagate(matrices[layer_index][0], matrices[layer_index][1], mixed_re, mixed_im)
        leave_re = wave_re.astype(jnp.float32)
        leave_im = wave_im.astype(jnp.float32)
        factor = 2.0 * (leave_re * leave_re + leave_im * leave_im - measured) * weights[:, None, None]
        back_re = (factor * leave_re).astype(jnp.bfloat16)
        back_im = (factor * leave_im).astype(jnp.bfloat16)
        patch_re = [None] * SLICES
        patch_im = [None] * SLICES
        for layer_index in reversed(range(SLICES)):
            matrix_re, matrix_im = matrices[layer_index]
            spread_re, spread_im = propagate(matrix_re.T, -matrix_im.T, back_re, back_im)
            enter_re, enter_im = entries[layer_index]
            patch_re[layer_index], patch_im[layer_index] = conj_times(enter_re, enter_im, spread_re, spread_im)
            if layer_index > 0:
                next_re, next_im = conj_times(windows[:, 0, layer_index], windows[:, 1, layer_index], spread_re, spread_im)
                back_re = next_re.astype(jnp.bfloat16)
                back_im = next_im.astype(jnp.bfloat16)
        patches = jnp.stack([jnp.stack(patch_re, axis=1), jnp.stack(patch_im, axis=1)], axis=1)
        for member in range(P_DEV):
            corner = (anchor, anchor, starts[member], col_offsets[member])
            current = lax.dynamic_slice(gradient, corner, (2, SLICES, WAVE, WAVE))
            gradient = lax.dynamic_update_slice(gradient, current + patches[member], corner)
        return (gradient, None)
    gradient, ignored = lax.scan(per_tile, gradient, jnp.arange(TILES, dtype=jnp.int32))
    return gradient[:, :, :NX]
```

```python
import functools
import math

import jax
import jax.numpy as jnp
import numpy as np
from jax import lax
from jax.experimental import pallas as pl
from jax.experimental.pallas import tpu as pltpu
from jax.sharding import PartitionSpec as P

BF = jnp.bfloat16
F32 = jnp.float32


def mm(a, b):
    return jnp.dot(a, b, preferred_element_type=F32)


def base_tables(n):
    product = np.outer(np.arange(n), np.arange(n)) % n
    angles = product * (2.0 * math.pi / n)
    return np.cos(angles), np.sin(angles)


def tables_kernel(phase_ref, cos_ref, sin_ref, near_left, near_right):
    n = cos_ref.shape[0]
    phase = jnp.broadcast_to(phase_ref[...], (8, n))
    turn = jnp.where(
        lax.broadcasted_iota(jnp.int32, (8, n), 0) == 0, jnp.cos(phase), jnp.sin(phase)
    )

    def exact(a, b):
        return jnp.dot(a, b, precision=lax.Precision.HIGHEST, preferred_element_type=F32)

    by_cos = exact(turn, cos_ref[...])
    by_sin = exact(turn, sin_ref[...])
    scale = 1.0 / n
    ahead_re = (by_cos[0:1] + by_sin[1:2]) * scale
    ahead_im = (by_cos[1:2] - by_sin[0:1]) * scale
    behind_re = (by_cos[0:1] - by_sin[1:2]) * scale
    behind_im = (by_cos[1:2] + by_sin[0:1]) * scale

    def circulant(row):
        return pltpu.roll(
            jnp.broadcast_to(row, (n, n)), 0, 1, stride=1, stride_axis=0
        ).astype(BF)

    m_re, m_im = circulant(ahead_re), circulant(ahead_im)
    t_re, t_im = circulant(behind_re), circulant(behind_im)
    near_left[:n, :n] = m_re
    near_left[:n, n:] = -m_im
    near_left[n:, :n] = m_im
    near_left[n:, n:] = m_re
    near_right[:n, :n] = t_re
    near_right[:n, n:] = t_im
    near_right[n:, :n] = -t_im
    near_right[n:, n:] = t_re


def propagate(left, right, waves_re, waves_im):
    n = waves_re[0].shape[0]
    count = len(waves_re)
    field = jnp.concatenate(
        [jnp.concatenate(waves_re, axis=1), jnp.concatenate(waves_im, axis=1)], axis=0
    )
    inner = mm(left, field).astype(BF)
    rows = [
        jnp.concatenate([inner[:n, w * n : (w + 1) * n], inner[n:, w * n : (w + 1) * n]], axis=1)
        for w in range(count)
    ]
    outer = mm(jnp.concatenate(rows, axis=0), right)
    return (
        [outer[w * n : (w + 1) * n, :n] for w in range(count)],
        [outer[w * n : (w + 1) * n, n:] for w in range(count)],
    )


def wave_kernel(
    own_set,
    meta_ref,
    here_ref,
    there_ref,
    probe_ref,
    own_int_ref,
    int_here_ref,
    int_there_ref,
    near_left,
    near_right,
    far_left,
    far_right,
    own_here_ref,
    own_there_ref,
    base_ref,
    out_ref,
    patch_re,
    patch_im,
):
    n = probe_ref.shape[1]
    slots = own_int_ref.shape[0]
    sec = meta_ref[2, 0]
    parity = meta_ref[2, 1]
    is_own = (parity == 0) if own_set else (parity != 0)
    which = jnp.where(is_own, 0, 1)
    rows = lax.broadcasted_iota(jnp.int32, (n, n), 0)
    cols = lax.broadcasted_iota(jnp.int32, (n, n), 1)
    top = sec == 0

    masks = []
    for w in range(slots):
        r = meta_ref[which, w]
        c = meta_ref[which, slots + w]
        at_or_past = (rows >= r).astype(jnp.int32)
        mine = at_or_past == jnp.where(is_own, 1, 0)
        masks.append((mine, cols >= c, r, c))
    live = meta_ref[which, 2 * slots]

    def planes(layer, part):
        def pick(a_ref, b_ref):
            a, b = a_ref[part, 0], b_ref[part, 0]
            return jnp.where(top if layer == 0 else jnp.logical_not(top), a, b).astype(F32)

        own = pick(own_here_ref, own_there_ref)
        other = pick(here_ref, there_ref)
        return [
            jnp.where(
                mine,
                jnp.where(left, own[:, :n], own[:, n:]),
                jnp.where(left, other[:, :n], other[:, n:]),
            )
            for mine, left, _, _ in masks
        ]

    def rolled(part):
        plane = probe_ref[part].astype(F32)
        return [pltpu.roll(pltpu.roll(plane, r, 0), c, 1) for _, _, r, c in masks]

    def to_bf(parts):
        return [p.astype(BF) for p in parts]

    def times(a_re, a_im, b_re, b_im):
        return (
            [ar * br - ai * bi for ar, ai, br, bi in zip(a_re, a_im, b_re, b_im)],
            [ar * bi + ai * br for ar, ai, br, bi in zip(a_re, a_im, b_re, b_im)],
        )

    def conj_times(a_re, a_im, b_re, b_im):
        return (
            [ar * br + ai * bi for ar, ai, br, bi in zip(a_re, a_im, b_re, b_im)],
            [ar * bi - ai * br for ar, ai, br, bi in zip(a_re, a_im, b_re, b_im)],
        )

    def rounded(parts):
        return [p.astype(BF).astype(F32) for p in parts]

    near_l, near_r = near_left[...], near_right[...]
    far_l, far_r = far_left[...], far_right[...]
    probe_re, probe_im = rolled(0), rolled(1)
    t_re, t_im = planes(0, 0), planes(0, 1)
    z_re, z_im = times(t_re, t_im, probe_re, probe_im)
    psi_re, psi_im = propagate(near_l, near_r, to_bf(z_re), to_bf(z_im))
    psi_re, psi_im = rounded(psi_re), rounded(psi_im)
    t_re, t_im = planes(1, 0), planes(1, 1)
    z_re, z_im = times(t_re, t_im, psi_re, psi_im)
    end_re, end_im = propagate(far_l, far_r, to_bf(z_re), to_bf(z_im))
    chi_re, chi_im = [], []
    for w in range(slots):
        received = jnp.where(
            top,
            jnp.concatenate([int_here_ref[w], int_there_ref[w]], axis=0),
            jnp.concatenate([int_there_ref[w], int_here_ref[w]], axis=0),
        )
        measured = jnp.where(is_own, own_int_ref[w], received).astype(F32)
        weight = jnp.where(w < live, 2.0, 0.0)
        factor = weight * (end_re[w] * end_re[w] + end_im[w] * end_im[w] - measured)
        chi_re.append(factor * end_re[w])
        chi_im.append(factor * end_im[w])
    y_re, y_im = propagate(far_r, far_l, to_bf(chi_re), to_bf(chi_im))
    y_re, y_im = rounded(y_re), rounded(y_im)

    def keep(a_re, a_im, b_re, b_im):
        parts_re, parts_im = conj_times(a_re, a_im, b_re, b_im)
        for w in range(slots):
            patch_re[w] = parts_re[w]
            patch_im[w] = parts_im[w]

    @pl.when(top)
    def _():
        g_re, g_im = conj_times(t_re, t_im, y_re, y_im)
        w_re, w_im = propagate(near_r, near_l, to_bf(g_re), to_bf(g_im))
        keep(probe_re, probe_im, rounded(w_re), rounded(w_im))

    @pl.when(jnp.logical_not(top))
    def _():
        keep(psi_re, psi_im, y_re, y_im)

    for part, patch in ((0, patch_re), (1, patch_im)):
        left_sum = base_ref[part, 0, :, :n] if base_ref is not None else jnp.zeros((n, n), F32)
        right_sum = base_ref[part, 0, :, n:] if base_ref is not None else jnp.zeros((n, n), F32)
        for w, (mine, left, _, _) in enumerate(masks):
            value = jnp.where(mine, patch[w], 0.0)
            left_sum = left_sum + jnp.where(left, value, 0.0)
            right_sum = right_sum + jnp.where(left, 0.0, value)
        out_ref[part, 0, :, :n] = left_sum
        out_ref[part, 0, :, n:] = right_sum


def first_kernel(meta, h, t, p, oi, ih, it, nl, nr, fl, fr, oh, ot, out, pr, pi):
    wave_kernel(True, meta, h, t, p, oi, ih, it, nl, nr, fl, fr, oh, ot, None, out, pr, pi)


def second_kernel(meta, h, t, p, oi, ih, it, nl, nr, fl, fr, oh, ot, base, out, pr, pi):
    wave_kernel(False, meta, h, t, p, oi, ih, it, nl, nr, fl, fr, oh, ot, base, out, pr, pi)


VM = pl.BlockSpec(memory_space=pltpu.VMEM)
SM = pl.BlockSpec(memory_space=pltpu.SMEM)


def on_device(obj, probe, phases, intensities, pos_row, pos_col, counts):
    n = probe.shape[1]
    slots = pos_row.shape[0]
    tiles = lax.axis_size("tile")
    sec = lax.axis_index("sec")
    tile = lax.axis_index("tile")
    parity = tile % 2

    def swap(value):
        return lax.ppermute(value, "sec", [(0, 1), (1, 0)])

    def send(value, pairs):
        return lax.ppermute(value, "tile", [(a, b) for a, b in pairs if 0 <= b < tiles])

    onward = [(i, i + 1) for i in range(tiles)]
    paired = [(i, i ^ 1) for i in range(tiles)]
    across = [(i, i + 1 if i % 2 else i - 1) for i in range(tiles)]

    facing = send(obj, paired)
    own_meta = jnp.concatenate([pos_row, pos_col, counts])
    past_meta = send(own_meta, onward)
    half = intensities.shape[1] // 2
    int_here = send(
        lax.dynamic_slice_in_dim(intensities, sec * half, half, 1), onward
    )
    own_there = swap(obj)
    cos_table, sin_table = base_tables(n)
    f_re, f_im = cos_table / math.sqrt(n), -sin_table / math.sqrt(n)
    far_left = jnp.asarray(np.block([[f_re, -f_im], [f_im, f_re]]), BF)
    far_right = jnp.asarray(np.block([[f_re, f_im], [-f_im, f_re]]), BF)
    double = jax.ShapeDtypeStruct((2 * n, 2 * n), BF)
    near_left, near_right = pl.pallas_call(
        tables_kernel,
        out_shape=(double, double),
        in_specs=[VM] * 3,
        out_specs=(VM, VM),
        name="tables",
    )(phases[None], jnp.asarray(cos_table, F32), jnp.asarray(sin_table, F32))
    later, near_left = lax.optimization_barrier((obj, near_left))
    opposite = send(later, across)
    facing_there = swap(facing)
    int_there = swap(int_here)
    opposite_there = swap(opposite)
    place = jnp.stack([sec, parity] + [jnp.zeros((), jnp.int32)] * (2 * slots - 1))
    meta = jnp.stack([own_meta, past_meta, place]).astype(jnp.int32)
    out_shape = jax.ShapeDtypeStruct(obj.shape, F32)
    scratch = [pltpu.VMEM((slots, n, n), F32)] * 2
    params = pltpu.CompilerParams(vmem_limit_bytes=40 * 1024 * 1024)
    shared = (probe, intensities, int_here, int_there, near_left, near_right, far_left, far_right, obj, own_there)
    partial = pl.pallas_call(
        first_kernel,
        out_shape=out_shape,
        in_specs=[SM] + [VM] * 12,
        out_specs=VM,
        scratch_shapes=scratch,
        compiler_params=params,
        name="facing_waves",
    )(meta, facing, facing_there, *shared)
    return pl.pallas_call(
        second_kernel,
        out_shape=out_shape,
        in_specs=[SM] + [VM] * 13,
        out_specs=VM,
        scratch_shapes=scratch,
        compiler_params=params,
        name="opposite_waves",
    )(meta, opposite, opposite_there, *shared, partial)


def solution(mesh):
    placed = (
        P(None, "sec", "tile", None),
        P(),
        P(),
        P("tile", None, None),
        P("tile"),
        P("tile"),
        P("tile"),
    )
    return jax.shard_map(
        on_device,
        mesh=mesh,
        in_specs=placed,
        out_specs=P(None, "sec", "tile", None),
        check_vma=False,
    )
```

```python
import math

import jax
import jax.numpy as jnp
import numpy as np
from jax import lax
from jax.experimental import pallas as pl
from jax.experimental.pallas import tpu as pltpu
from jax.sharding import PartitionSpec as P

BF = jnp.bfloat16
F32 = jnp.float32
VM = pl.BlockSpec(memory_space=pltpu.VMEM)
SM = pl.BlockSpec(memory_space=pltpu.SMEM)
MIB = 1024 * 1024
CODE_ROWS = 16
TINY = pl.CostEstimate(flops=1000, bytes_accessed=1000, transcendentals=0)


def mm(a, b):
    return jnp.dot(a, b, preferred_element_type=F32)


def in_top():
    return lax.axis_index("sec") == 0


def owned(which_set):
    return lax.axis_index("tile") % 2 == which_set


def message_kernel(row_ref, col_ref, count_ref, ints_ref, strip_ref, out, second):
    second[...] = strip_ref[1:2]
    slots, size, n = out.shape
    half = size - CODE_ROWS
    start = pl.multiple_of(lax.axis_index("sec") * half, half)
    out[:, :half, :] = ints_ref[:, pl.ds(start, half), :]
    at_row = lax.broadcasted_iota(jnp.int32, (CODE_ROWS, n), 0)
    values = [row_ref[w] for w in range(slots)] + [col_ref[w] for w in range(slots)]
    codes = jnp.zeros((CODE_ROWS, n), F32)
    for k, value in enumerate(values + [count_ref[0]]):
        codes = jnp.where(at_row == k, value.astype(F32), codes)
    for w in range(slots):
        out[w, half:, :] = codes.astype(BF)


def place_waves(corners, live, own, probe_ref, own_here, own_there, marks, rolled, seen):
    n = probe_ref.shape[1]
    rows = lax.broadcasted_iota(jnp.int32, (n, n), 0)
    cols = lax.broadcasted_iota(jnp.int32, (n, n), 1)
    at_row = lax.broadcasted_iota(jnp.int32, (8, n), 0)
    top = in_top()
    for w, (r, c) in enumerate(corners):
        weight = jnp.where(w < live, 2, 0)
        signed = r if own else -r
        marks[w] = jnp.where(at_row == 0, signed, jnp.where(at_row == 1, c, weight))
        mine, left = (rows >= r) if own else (rows < r), cols >= c
        for part in range(2):
            plane = pltpu.roll(probe_ref[part].astype(F32), r, 0)
            rolled[w, part] = pltpu.roll(plane, c, 1).astype(BF)

            def choose(ref):
                plane = ref[part, 0].astype(F32)
                both = jnp.where(left, plane[:, :n], plane[:, n:])
                return jnp.where(mine, both, 0.0).astype(BF)

            here, there = choose(own_here), choose(own_there)

            @pl.when(top)
            def _():
                seen[w, 0, part] = here
                seen[w, 1, part] = there

            @pl.when(jnp.logical_not(top))
            def _():
                seen[w, 0, part] = there
                seen[w, 1, part] = here


def own_kernel(
    row_ref, col_ref, count_ref, phase_ref, probe_ref, own_here, own_there,
    near_left, near_right, far_left, far_right, marks, rolled, seen,
):
    n = probe_ref.shape[1]
    slots = rolled.shape[0]
    phase = jnp.broadcast_to(phase_ref[...], (8, n))
    turn = jnp.where(
        lax.broadcasted_iota(jnp.int32, (8, n), 0) == 0, jnp.cos(phase), jnp.sin(phase)
    )

    def exact(a, b):
        return jnp.dot(a, b, precision=lax.Precision.HIGHEST, preferred_element_type=F32)

    product = lax.broadcasted_iota(jnp.int32, (n, n), 0) * lax.broadcasted_iota(
        jnp.int32, (n, n), 1
    )
    angles = lax.rem(product, n).astype(F32) * (2.0 * math.pi / n)
    cosine, sine = jnp.cos(angles), jnp.sin(angles)
    by_cos = exact(turn, cosine)
    by_sin = exact(turn, sine)
    scale = 1.0 / n

    def circulant(row):
        return pltpu.roll(
            jnp.broadcast_to(row * scale, (n, n)), 0, 1, stride=1, stride_axis=0
        ).astype(BF)

    m_re, m_im = circulant(by_cos[0:1] + by_sin[1:2]), circulant(by_cos[1:2] - by_sin[0:1])
    t_re, t_im = circulant(by_cos[0:1] - by_sin[1:2]), circulant(by_cos[1:2] + by_sin[0:1])
    f_re, f_im = (cosine / math.sqrt(n)).astype(BF), (-sine / math.sqrt(n)).astype(BF)

    def fill(table, re, im, low):
        table[:n, :n] = re
        table[n:, n:] = re
        table[:n, n:] = -im if low else im
        table[n:, :n] = im if low else -im

    fill(near_left, m_re, m_im, True)
    fill(near_right, t_re, t_im, False)
    fill(far_left, f_re, f_im, True)
    fill(far_right, f_re, f_im, False)
    corners = [(row_ref[w], col_ref[w]) for w in range(slots)]
    place_waves(
        corners, count_ref[0], True, probe_ref, own_here, own_there, marks, rolled, seen
    )


def past_kernel(received, probe_ref, own_here, own_there, marks, rolled, seen):
    slots, n = rolled.shape[0], rolled.shape[2]
    height = received.shape[1] - CODE_ROWS
    codes = received[0, height:].astype(F32)
    at_row = lax.broadcasted_iota(jnp.int32, codes.shape, 0)

    def decode(k):
        return jnp.max(jnp.where(at_row == k, codes, 0.0)).astype(jnp.int32)

    corners = [(decode(w), decode(slots + w)) for w in range(slots)]
    place_waves(
        corners, decode(2 * slots), False, probe_ref, own_here, own_there, marks, rolled, seen
    )


def propagate(left, right, field, inner, outer):
    n = inner.shape[1] // 2
    count = field.shape[1] // n
    product = mm(left[...], field[...]).astype(BF)
    for w in range(count):
        inner[w * n : (w + 1) * n, :n] = product[:n, w * n : (w + 1) * n]
        inner[w * n : (w + 1) * n, n:] = product[n:, w * n : (w + 1) * n]
    outer[...] = mm(inner[...], right[...])


class Waves:
    def __init__(self, which_set, placed, near, far, field, inner, outer):
        own = owned(which_set)
        self.own, self.near, self.far = own, near, far
        self.slots, _, self.n, _ = placed[1].shape
        n = self.n
        self.placed = placed
        self.field, self.inner, self.outer = field, inner, outer
        flip = jnp.where(own, 0, -1)
        rows = lax.broadcasted_iota(jnp.int32, (n, n), 0) ^ flip
        cols = lax.broadcasted_iota(jnp.int32, (n, n), 1)
        self.marks = [self.pick(0, w) for w in range(self.slots)]
        self.masks = [(rows >= mark[0:1], cols >= mark[1:2]) for mark in self.marks]

    def pick(self, kind, *at):
        return jnp.where(self.own, self.placed[kind][at], self.placed[3 + kind][at])

    def window(self, w, layer, other):
        mine, left = self.masks[w]
        planes = []
        for part in range(2):
            plane = jnp.concatenate([piece[0] for piece in other[part]], axis=0).astype(F32)
            outside = jnp.where(left, plane[:, : self.n], plane[:, self.n :])
            planes.append(jnp.where(mine, self.pick(2, w, layer, part).astype(F32), outside))
        return planes

    def probe(self, w):
        return [self.pick(1, w, part).astype(F32) for part in range(2)]

    def put(self, w, re, im):
        n = self.n
        self.field[:n, w * n : (w + 1) * n] = re.astype(BF)
        self.field[n:, w * n : (w + 1) * n] = im.astype(BF)

    def got(self, w):
        n = self.n
        return self.outer[w * n : (w + 1) * n, :n], self.outer[w * n : (w + 1) * n, n:]

    def forward(self, mats):
        propagate(mats[0], mats[1], self.field, self.inner, self.outer)

    def adjoint(self, mats):
        propagate(mats[1], mats[0], self.field, self.inner, self.outer)

    def enter(self, other, psi):
        for w in range(self.slots):
            t_re, t_im = self.window(w, 0, other)
            p_re, p_im = self.probe(w)
            self.put(w, t_re * p_re - t_im * p_im, t_re * p_im + t_im * p_re)
        self.forward(self.near)
        for w in range(self.slots):
            psi[w] = jnp.stack(self.got(w)).astype(BF)

    def leave(self, other, psi, own_int, int_here, int_there, back):
        for w in range(self.slots):
            t_re, t_im = self.window(w, 1, other)
            p_re, p_im = psi[w, 0].astype(F32), psi[w, 1].astype(F32)
            self.put(w, t_re * p_re - t_im * p_im, t_re * p_im + t_im * p_re)
        self.forward(self.far)
        n = self.n
        top = in_top()
        for w in range(self.slots):
            re, im = self.got(w)
            near, away = int_here[w, : n // 2].astype(F32), int_there[w, : n // 2].astype(F32)
            first, second = jnp.where(top, near, away), jnp.where(top, away, near)
            measured = jnp.where(
                self.own, own_int[w].astype(F32), jnp.concatenate([first, second], axis=0)
            )
            weight = self.marks[w][2:3].astype(F32)
            factor = weight * (re * re + im * im - measured)
            self.put(w, factor * re, factor * im)
        self.adjoint(self.far)
        for w in range(self.slots):
            back[w] = jnp.stack(self.got(w)).astype(BF)

    def reach_first(self, other, back):
        for w in range(self.slots):
            t_re, t_im = self.window(w, 1, other)
            y_re, y_im = back[w, 0].astype(F32), back[w, 1].astype(F32)
            self.put(w, t_re * y_re + t_im * y_im, t_re * y_im - t_im * y_re)
        self.adjoint(self.near)
        for w in range(self.slots):
            back[w] = jnp.stack(self.got(w)).astype(BF)

    def gradient(self, entering, back, base, out):
        n = self.n
        for part in range(2):
            sums = [0.0, 0.0] if base is None else [base[part, 0, :, :n], base[part, 0, :, n:]]
            for w in range(self.slots):
                mine, left = self.masks[w]
                a_re, a_im = entering(w)
                y_re, y_im = back[w, 0].astype(F32), back[w, 1].astype(F32)
                value = a_re * y_re + a_im * y_im if part == 0 else a_re * y_im - a_im * y_re
                value = jnp.where(mine, value, 0.0)
                sums[0] = sums[0] + jnp.where(left, value, 0.0)
                sums[1] = sums[1] + jnp.where(left, 0.0, value)
            out[part, 0, :, :n] = sums[0]
            out[part, 0, :, n:] = sums[1]


def facing_kernel(
    here_re, here_im, there_re0, there_re1, there_im0, there_im1, own_int, int_here, int_there, nl, nr, fl, fr, m0, r0, s0, m1, r1, s1,
    out, field, inner, outer, psi, back,
):
    waves = Waves(0, (m0, r0, s0, m1, r1, s1), (nl, nr), (fl, fr), field, inner, outer)
    top = in_top()
    ints = (own_int, int_here, int_there)
    here = [[here_re.at[0]], [here_im.at[0]]]
    there = [[there_re0.at[0], there_re1.at[0]], [there_im0.at[0], there_im1.at[0]]]

    @pl.when(top)
    def _():
        waves.enter(here, psi)
        waves.leave(there, psi, *ints, back)
        waves.reach_first(there, back)
        waves.gradient(waves.probe, back, None, out)

    @pl.when(jnp.logical_not(top))
    def _():
        waves.enter(there, psi)
        waves.leave(here, psi, *ints, back)
        waves.gradient(lambda w: psi[w].astype(F32), back, None, out)


def entering_kernel(here_re, here_im, nl, nr, m0, r0, s0, m1, r1, s1, psi, field, inner, outer):
    @pl.when(in_top())
    def _():
        waves = Waves(1, (m0, r0, s0, m1, r1, s1), (nl, nr), None, field, inner, outer)
        waves.enter([[here_re.at[0]], [here_im.at[0]]], psi)


def opposite_kernel(
    here_re, here_im, there_re, there_im, own_int, int_here, int_there, nl, nr, fl, fr, m0, r0, s0, m1, r1, s1,
    entered, base, out, field, inner, outer, psi, back,
):
    waves = Waves(1, (m0, r0, s0, m1, r1, s1), (nl, nr), (fl, fr), field, inner, outer)
    ints = (own_int, int_here, int_there)
    here, there = [[here_re.at[0]], [here_im.at[0]]], [[there_re.at[0]], [there_im.at[0]]]
    top = in_top()

    @pl.when(top)
    def _():
        waves.leave(there, entered, *ints, back)
        waves.reach_first(there, back)
        waves.gradient(waves.probe, back, base, out)

    @pl.when(jnp.logical_not(top))
    def _():
        waves.enter(there, psi)
        waves.leave(here, psi, *ints, back)
        waves.gradient(lambda w: psi[w].astype(F32), back, base, out)


def kernel_call(kernel, name, out_shape, in_specs, scratch_shapes=()):
    many = isinstance(out_shape, tuple)
    return pl.pallas_call(
        kernel,
        out_shape=out_shape,
        in_specs=in_specs,
        out_specs=(VM,) * len(out_shape) if many else VM,
        scratch_shapes=scratch_shapes,
        compiler_params=pltpu.CompilerParams(vmem_limit_bytes=16 * MIB),
        cost_estimate=TINY,
        name=name,
    )


def on_device(obj, probe, phases, intensities, pos_row, pos_col, counts):
    n = probe.shape[1]
    slots = pos_row.shape[0]
    tiles = lax.axis_size("tile")
    half = intensities.shape[1] // lax.axis_size("sec")
    after = lax.optimization_barrier

    def swap(value):
        return lax.ppermute(value, "sec", [(0, 1), (1, 0)])

    def send(value, pairs):
        return lax.ppermute(value, "tile", [(a, b) for a, b in pairs if 0 <= b < tiles])

    onward = [(i, i + 1) for i in range(tiles)]
    paired = [(i, i ^ 1) for i in range(tiles)]
    across = [(i, i + 1 if i % 2 else i - 1) for i in range(tiles)]
    relayed = [(i, i - 2 if i % 2 else i + 2) for i in range(tiles)]

    facing_re = send(obj[0:1], paired)
    own_there = swap(obj)
    positions = (pos_row, pos_col, counts)
    cut = (1, *obj.shape[1:])
    message, second = kernel_call(
        message_kernel,
        "message",
        (
            jax.ShapeDtypeStruct((slots, half + CODE_ROWS, n), BF),
            jax.ShapeDtypeStruct(cut, BF),
        ),
        [SM] * 3 + [VM] * 2,
    )(*positions, intensities, obj)
    facing_im = send(second, paired)
    int_here = send(message, onward)
    opposite_re = send(facing_re, relayed)
    direct, _ = after((second, facing_re))
    opposite_im = send(direct, across)
    phases, _ = after((phases, facing_re))

    double = jax.ShapeDtypeStruct((2 * n, 2 * n), BF)
    wave_shapes = (
        jax.ShapeDtypeStruct((slots, 8, n), jnp.int32),
        jax.ShapeDtypeStruct((slots, 2, n, n), BF),
        jax.ShapeDtypeStruct((slots, 2, 2, n, n), BF),
    )
    nl, nr, fl, fr, *own_waves = kernel_call(
        own_kernel, "own", (double,) * 4 + wave_shapes, [SM] * 3 + [VM] * 4
    )(*positions, phases[None], probe, obj, own_there)
    int_here, nl = after((int_here, nl))
    int_there = swap(int_here)
    past_waves = kernel_call(past_kernel, "past", wave_shapes, [VM] * 4)(
        int_here, probe, obj, own_there
    )
    placed = (*own_waves, *past_waves)

    work = [
        pltpu.VMEM((2 * n, slots * n), BF),
        pltpu.VMEM((slots * n, 2 * n), BF),
        pltpu.VMEM((slots * n, 2 * n), F32),
    ]
    def pieces(value):
        middle = value.shape[2] // 2
        return swap(value[:, :, :middle]), swap(value[:, :, middle:])

    pair = pltpu.VMEM((slots, 2, n, n), BF)
    own_ints, opposite_re = after((intensities, opposite_re))
    ints = (own_ints, int_here, int_there)
    grad_shape = jax.ShapeDtypeStruct(obj.shape, F32)
    partial = kernel_call(
        facing_kernel, "facing", grad_shape, [VM] * 19, work + [pair, pair]
    )(facing_re, facing_im, *pieces(facing_re), *pieces(facing_im), *ints, nl, nr, fl, fr, *placed)
    opposite_re, opposite_im, partial = after((opposite_re, opposite_im, partial))
    opposite = (opposite_re, opposite_im)
    opposite_there = (swap(opposite_re), swap(opposite_im))
    entered = kernel_call(
        entering_kernel, "entering", jax.ShapeDtypeStruct((slots, 2, n, n), BF), [VM] * 10, work
    )(*opposite, nl, nr, *placed)
    return kernel_call(
        opposite_kernel, "opposite", grad_shape, [VM] * 19, work + [pair, pair]
    )(*opposite, *opposite_there, *ints, nl, nr, fl, fr, *placed, entered, partial)


def solution(mesh):
    placed = (
        P(None, "sec", "tile", None),
        P(),
        P(),
        P("tile", None, None),
        P("tile"),
        P("tile"),
        P("tile"),
    )
    return jax.shard_map(
        on_device,
        mesh=mesh,
        in_specs=placed,
        out_specs=P(None, "sec", "tile", None),
        check_vma=False,
    )
```

```python
import math

import jax
import jax.numpy as jnp
import numpy as np
from jax import lax
from jax.experimental import pallas as pl
from jax.experimental.pallas import tpu as pltpu
from jax.sharding import PartitionSpec as P

BF = jnp.bfloat16
F32 = jnp.float32
VM = pl.BlockSpec(memory_space=pltpu.VMEM)
SM = pl.BlockSpec(memory_space=pltpu.SMEM)
MIB = 1024 * 1024
CODE_ROWS = 16
STEP = 32
SENT = 64
TINY = pl.CostEstimate(flops=1000, bytes_accessed=1000, transcendentals=0)


def mm(a, b):
    return jnp.dot(a, b, preferred_element_type=F32)


def in_top():
    return lax.axis_index("sec") == 0


def owned(which_set):
    return lax.axis_index("tile") % 2 == which_set


def message_kernel(row_ref, col_ref, count_ref, ints_ref, strip_ref, out, second):
    second[...] = strip_ref[1:2]
    slots, size, n = out.shape
    half = size - CODE_ROWS
    start = pl.multiple_of(lax.axis_index("sec") * half, half)
    out[:, :half, :] = ints_ref[:, pl.ds(start, half), :]
    at_row = lax.broadcasted_iota(jnp.int32, (CODE_ROWS, n), 0)
    values = [row_ref[w] for w in range(slots)] + [col_ref[w] for w in range(slots)]
    codes = jnp.zeros((CODE_ROWS, n), F32)
    for k, value in enumerate(values + [count_ref[0]]):
        codes = jnp.where(at_row == k, value.astype(F32), codes)
    for w in range(slots):
        out[w, half:, :] = codes.astype(BF)


def place_waves(corners, live, own, probe_ref, own_here, own_there, marks, rolled, seen):
    n = probe_ref.shape[1]
    rows = lax.broadcasted_iota(jnp.int32, (n, n), 0)
    cols = lax.broadcasted_iota(jnp.int32, (n, n), 1)
    at_row = lax.broadcasted_iota(jnp.int32, (8, n), 0)
    top = in_top()
    for w, (r, c) in enumerate(corners):
        weight = jnp.where(w < live, 2, 0)
        signed = r if own else -r
        marks[w] = jnp.where(at_row == 0, signed, jnp.where(at_row == 1, c, weight))
        mine, left = (rows >= r) if own else (rows < r), cols >= c
        for part in range(2):
            plane = pltpu.roll(probe_ref[part].astype(F32), r, 0)
            rolled[w, part] = pltpu.roll(plane, c, 1).astype(BF)

            def choose(ref):
                plane = ref[part, 0].astype(F32)
                both = jnp.where(left, plane[:, :n], plane[:, n:])
                return jnp.where(mine, both, 0.0).astype(BF)

            here, there = choose(own_here), choose(own_there)

            @pl.when(top)
            def _():
                seen[w, 0, part] = here
                seen[w, 1, part] = there

            @pl.when(jnp.logical_not(top))
            def _():
                seen[w, 0, part] = there
                seen[w, 1, part] = here


def own_kernel(
    row_ref, col_ref, count_ref, phase_ref, probe_ref, own_here, own_there,
    near_left, near_right, far_left, far_right, marks, rolled, seen,
):
    n = probe_ref.shape[1]
    slots = rolled.shape[0]
    phase = jnp.broadcast_to(phase_ref[...], (8, n))
    turn = jnp.where(
        lax.broadcasted_iota(jnp.int32, (8, n), 0) == 0, jnp.cos(phase), jnp.sin(phase)
    )

    def exact(a, b):
        return jnp.dot(a, b, precision=lax.Precision.HIGHEST, preferred_element_type=F32)

    product = lax.broadcasted_iota(jnp.int32, (n, n), 0) * lax.broadcasted_iota(
        jnp.int32, (n, n), 1
    )
    angles = lax.rem(product, n).astype(F32) * (2.0 * math.pi / n)
    cosine, sine = jnp.cos(angles), jnp.sin(angles)
    by_cos = exact(turn, cosine)
    by_sin = exact(turn, sine)
    scale = 1.0 / n

    def circulant(row):
        return pltpu.roll(
            jnp.broadcast_to(row * scale, (n, n)), 0, 1, stride=1, stride_axis=0
        ).astype(BF)

    m_re, m_im = circulant(by_cos[0:1] + by_sin[1:2]), circulant(by_cos[1:2] - by_sin[0:1])
    t_re, t_im = circulant(by_cos[0:1] - by_sin[1:2]), circulant(by_cos[1:2] + by_sin[0:1])
    f_re, f_im = (cosine / math.sqrt(n)).astype(BF), (-sine / math.sqrt(n)).astype(BF)

    def fill(table, re, im, low):
        table[:n, :n] = re
        table[n:, n:] = re
        table[:n, n:] = -im if low else im
        table[n:, :n] = im if low else -im

    fill(near_left, m_re, m_im, True)
    fill(near_right, t_re, t_im, False)
    fill(far_left, f_re, f_im, True)
    fill(far_right, f_re, f_im, False)
    corners = [(row_ref[w], col_ref[w]) for w in range(slots)]
    place_waves(
        corners, count_ref[0], True, probe_ref, own_here, own_there, marks, rolled, seen
    )


def past_kernel(received, probe_ref, own_here, own_there, marks, rolled, seen):
    slots, n = rolled.shape[0], rolled.shape[2]
    height = received.shape[1] - CODE_ROWS
    codes = received[0, height:].astype(F32)
    at_row = lax.broadcasted_iota(jnp.int32, codes.shape, 0)

    def decode(k):
        return jnp.max(jnp.where(at_row == k, codes, 0.0)).astype(jnp.int32)

    corners = [(decode(w), decode(slots + w)) for w in range(slots)]
    place_waves(
        corners, decode(2 * slots), False, probe_ref, own_here, own_there, marks, rolled, seen
    )


class Waves:
    def __init__(self, which_set, placed, near, far, work):
        self.placed, self.near, self.far = placed, near, far
        self.field, self.inner, self.outer, self.last = work
        self.slots, _, self.n, _ = placed[1].shape
        self.own = owned(which_set)
        self.flip = jnp.where(self.own, 0, -1)
        self.marks = [self.pick(0, w) for w in range(self.slots)]
        cols = lax.broadcasted_iota(jnp.int32, (STEP, self.n), 1)
        self.left = [cols >= mark[1:2] for mark in self.marks]

    def pick(self, kind, *at):
        return jnp.where(self.own, self.placed[kind][at], self.placed[3 + kind][at])

    def rows(self):
        return [slice(at, at + STEP) for at in range(0, self.n, STEP)]

    def mine(self, w, at):
        index = lax.broadcasted_iota(jnp.int32, (STEP, self.n), 0) + at.start
        return (index ^ self.flip) >= self.marks[w][0:1]

    def window(self, w, layer, other, at):
        n = self.n
        mine, left = self.mine(w, at), self.left[w]
        planes = []
        for part in range(2):
            pieces = other[part]
            size = n // len(pieces)
            piece, first = pieces[at.start // size], at.start % size
            plane = piece[0, first : first + STEP, :].astype(F32)
            outside = jnp.where(left, plane[:, :n], plane[:, n:])
            inside = self.pick(2, w, layer, part, at).astype(F32)
            planes.append(jnp.where(mine, inside, outside))
        return planes

    def probe(self, w, at):
        return [self.pick(1, w, part, at).astype(F32) for part in range(2)]

    def pair(self, ref, w, at):
        return ref[w, 0, at, :].astype(F32), ref[w, 1, at, :].astype(F32)

    def put(self, w, at, re, im):
        n = self.n
        lower = slice(n + at.start, n + at.stop)
        self.field[at, w * n : (w + 1) * n] = re.astype(BF)
        self.field[lower, w * n : (w + 1) * n] = im.astype(BF)

    def got(self, w, at):
        n = self.n
        here = slice(w * n + at.start, w * n + at.stop)
        return self.outer[here, :n], self.outer[here, n:]

    def propagate(self, left, right):
        n = self.n
        for w in range(self.slots):
            product = mm(left[...], self.field[:, w * n : (w + 1) * n]).astype(BF)
            self.inner[w * n : (w + 1) * n, :n] = product[:n]
            self.inner[w * n : (w + 1) * n, n:] = product[n:]
        for w in range(self.slots):
            here = slice(w * n, (w + 1) * n)
            self.outer[here, :] = mm(self.inner[here, :], right[...])

    def enter(self, other, psi):
        for w in range(self.slots):
            for at in self.rows():
                t_re, t_im = self.window(w, 0, other, at)
                p_re, p_im = self.probe(w, at)
                self.put(w, at, t_re * p_re - t_im * p_im, t_re * p_im + t_im * p_re)
        self.propagate(*self.near)
        for w in range(self.slots):
            for at in self.rows():
                re, im = self.got(w, at)
                psi[w, 0, at, :] = re.astype(BF)
                psi[w, 1, at, :] = im.astype(BF)

    def leave(self, other, psi, own_int, int_here, int_there):
        for w in range(self.slots):
            for at in self.rows():
                t_re, t_im = self.window(w, 1, other, at)
                self.last[w, 0, at, :] = t_re.astype(BF)
                self.last[w, 1, at, :] = t_im.astype(BF)
                p_re, p_im = self.pair(psi, w, at)
                self.put(w, at, t_re * p_re - t_im * p_im, t_re * p_im + t_im * p_re)
        self.propagate(*self.far)
        half = self.n // 2
        top = in_top()
        for w in range(self.slots):
            weight = self.marks[w][2:3].astype(F32)
            for at in self.rows():
                re, im = self.got(w, at)
                part = slice(at.start % half, at.start % half + STEP)
                is_here = top == (at.start < half)
                received = jnp.where(
                    is_here, int_here[w, part, :].astype(F32), int_there[w, part, :].astype(F32)
                )
                measured = jnp.where(self.own, own_int[w, at, :].astype(F32), received)
                factor = weight * (re * re + im * im - measured)
                self.put(w, at, factor * re, factor * im)
        self.propagate(self.far[1], self.far[0])

    def reach_first(self):
        for w in range(self.slots):
            for at in self.rows():
                t_re, t_im = self.pair(self.last, w, at)
                y_re, y_im = (part.astype(BF).astype(F32) for part in self.got(w, at))
                self.put(w, at, t_re * y_re + t_im * y_im, t_re * y_im - t_im * y_re)
        self.propagate(self.near[1], self.near[0])

    def gradient(self, entering, base, out, final=None, sems=None):
        n = self.n
        copies = []
        for at in self.rows():
            sums = [0.0] * 4
            if base is not None:
                sums = [base[part, 0, at, c : c + n] for part in range(2) for c in (0, n)]
            for w in range(self.slots):
                mine, left = self.mine(w, at), self.left[w]
                a_re, a_im = entering(w, at)
                y_re, y_im = (part.astype(BF).astype(F32) for part in self.got(w, at))
                values = (a_re * y_re + a_im * y_im, a_re * y_im - a_im * y_re)
                for part, value in enumerate(values):
                    value = jnp.where(mine, value, 0.0)
                    first = jnp.where(left, value, 0.0)
                    sums[2 * part] = sums[2 * part] + first
                    sums[2 * part + 1] = sums[2 * part + 1] + (value - first)
            for part in range(2):
                out[part, 0, at, :n] = sums[2 * part]
                out[part, 0, at, n:] = sums[2 * part + 1]
            if final is not None and at.stop % SENT == 0:
                done = slice(at.stop - SENT, at.stop)
                copy = pltpu.make_async_copy(
                    out.at[:, :, done, :], final.at[:, :, done, :], sems.at[len(copies)]
                )
                copy.start()
                copies.append(copy)
        for copy in copies:
            copy.wait()


def facing_kernel(
    here_re, here_im, there_re, there_im, own_int, int_here, int_there, nl, nr, fl, fr,
    m0, r0, s0, m1, r1, s1, out, field, inner, outer, last, psi,
):
    placed = (m0, r0, s0, m1, r1, s1)
    waves = Waves(0, placed, (nl, nr), (fl, fr), (field, inner, outer, last))
    ints = (own_int, int_here, int_there)
    here, there = [[here_re.at[0]], [here_im.at[0]]], [[there_re.at[0]], [there_im.at[0]]]
    top = in_top()

    @pl.when(top)
    def _():
        waves.enter(here, psi)
        waves.leave(there, psi, *ints)
        waves.reach_first()
        waves.gradient(waves.probe, None, out)

    @pl.when(jnp.logical_not(top))
    def _():
        waves.enter(there, psi)
        waves.leave(here, psi, *ints)
        waves.gradient(lambda w, at: waves.pair(psi, w, at), None, out)


def entering_kernel(
    here_re, here_im, nl, nr, m0, r0, s0, m1, r1, s1, psi, field, inner, outer, last
):
    @pl.when(in_top())
    def _():
        placed = (m0, r0, s0, m1, r1, s1)
        waves = Waves(1, placed, (nl, nr), None, (field, inner, outer, last))
        waves.enter([[here_re.at[0]], [here_im.at[0]]], psi)


def opposite_kernel(
    here_re, here_im, there_re, there_im, own_int, int_here, int_there, nl, nr, fl, fr,
    m0, r0, s0, m1, r1, s1, entered, base, out, field, inner, outer, last, psi, total, sems,
):
    placed = (m0, r0, s0, m1, r1, s1)
    waves = Waves(1, placed, (nl, nr), (fl, fr), (field, inner, outer, last))
    ints = (own_int, int_here, int_there)
    here, there = [[here_re.at[0]], [here_im.at[0]]], [[there_re.at[0]], [there_im.at[0]]]
    top = in_top()

    @pl.when(top)
    def _():
        waves.leave(there, entered, *ints)
        waves.reach_first()
        waves.gradient(waves.probe, base, total, out, sems)

    @pl.when(jnp.logical_not(top))
    def _():
        waves.enter(there, psi)
        waves.leave(here, psi, *ints)
        waves.gradient(lambda w, at: waves.pair(psi, w, at), base, total, out, sems)


def kernel_call(kernel, name, out_shape, in_specs, scratch_shapes=(), out_spec=VM):
    many = isinstance(out_shape, tuple)
    return pl.pallas_call(
        kernel,
        out_shape=out_shape,
        in_specs=in_specs,
        out_specs=(VM,) * len(out_shape) if many else out_spec,
        scratch_shapes=scratch_shapes,
        compiler_params=pltpu.CompilerParams(vmem_limit_bytes=16 * MIB),
        cost_estimate=TINY,
        name=name,
    )


def on_device(obj, probe, phases, intensities, pos_row, pos_col, counts):
    n = probe.shape[1]
    slots = pos_row.shape[0]
    tiles = lax.axis_size("tile")
    half = intensities.shape[1] // lax.axis_size("sec")
    after = lax.optimization_barrier

    def swap(value):
        return lax.ppermute(value, "sec", [(0, 1), (1, 0)])

    def send(value, pairs):
        inside = [(a, b) for a, b in pairs if 0 <= min(a, b) and max(a, b) < tiles]
        return lax.ppermute(value, "tile", inside)

    onward = [(i, i + 1) for i in range(tiles)]
    paired = [(i, i ^ 1) for i in range(tiles)]
    relayed = [(i, i - 2 if i % 2 else i + 2) for i in range(tiles)]

    sideways = [(b, a) for a, b in relayed]
    facing_re = send(obj[0:1], paired)
    crossed = send(obj[1:2], sideways)
    opposite_im = send(crossed, paired)
    own_there = swap(obj)
    positions = (pos_row, pos_col, counts)
    cut = (1, *obj.shape[1:])
    message, second = kernel_call(
        message_kernel,
        "message",
        (
            jax.ShapeDtypeStruct((slots, half + CODE_ROWS, n), BF),
            jax.ShapeDtypeStruct(cut, BF),
        ),
        [SM] * 3 + [VM] * 2,
    )(*positions, intensities, obj)
    facing_im = send(second, paired)
    int_here = send(message, onward)
    opposite_re = send(facing_re, relayed)
    phases, _ = after((phases, facing_re))

    double = jax.ShapeDtypeStruct((2 * n, 2 * n), BF)
    wave_shapes = (
        jax.ShapeDtypeStruct((slots, 8, n), jnp.int32),
        jax.ShapeDtypeStruct((slots, 2, n, n), BF),
        jax.ShapeDtypeStruct((slots, 2, 2, n, n), BF),
    )
    nl, nr, fl, fr, *own_waves = kernel_call(
        own_kernel, "own", (double,) * 4 + wave_shapes, [SM] * 3 + [VM] * 4
    )(*positions, phases[None], probe, obj, own_there)
    facing_im, nl = after((facing_im, nl))
    int_here, _ = after((int_here, facing_im))
    int_there = swap(int_here)
    past_waves = kernel_call(past_kernel, "past", wave_shapes, [VM] * 4)(
        int_here, probe, obj, own_there
    )
    placed = (*own_waves, *past_waves)

    work = [
        pltpu.VMEM((2 * n, slots * n), BF),
        pltpu.VMEM((slots * n, 2 * n), BF),
        pltpu.VMEM((slots * n, 2 * n), F32),
    ]
    def pieces(value):
        middle = value.shape[2] // 2
        return swap(value[:, :, :middle]), swap(value[:, :, middle:])

    pair = pltpu.VMEM((slots, 2, n, n), BF)
    work.append(pair)
    ints = (intensities, int_here, int_there)
    grad_shape = jax.ShapeDtypeStruct(obj.shape, F32)
    partial = kernel_call(
        facing_kernel, "facing", grad_shape, [VM] * 17, work + [pair]
    )(facing_re, facing_im, swap(facing_re), swap(facing_im), *ints, nl, nr, fl, fr, *placed)
    opposite_re_there = swap(opposite_re)
    opposite_im, partial = after((opposite_im, partial))
    opposite = (opposite_re, opposite_im)
    opposite_there = (opposite_re_there, swap(opposite_im))
    entered = kernel_call(
        entering_kernel, "entering", jax.ShapeDtypeStruct((slots, 2, n, n), BF), [VM] * 10, work
    )(*opposite, nl, nr, *placed)
    return kernel_call(
        opposite_kernel,
        "opposite",
        grad_shape,
        [VM] * 19,
        work + [pair, pltpu.VMEM(obj.shape, F32), pltpu.SemaphoreType.DMA((n // SENT,))],
        out_spec=pl.BlockSpec(memory_space=pltpu.HBM),
    )(*opposite, *opposite_there, *ints, nl, nr, fl, fr, *placed, entered, partial)


def solution(mesh):
    placed = (
        P(None, "sec", "tile", None),
        P(),
        P(),
        P("tile", None, None),
        P("tile"),
        P("tile"),
        P("tile"),
    )
    return jax.shard_map(
        on_device,
        mesh=mesh,
        in_specs=placed,
        out_specs=P(None, "sec", "tile", None),
        check_vma=False,
    )
```

```python
import math

import jax
import jax.numpy as jnp
import numpy as np
from jax import lax
from jax.experimental import pallas as pl
from jax.experimental.pallas import tpu as pltpu
from jax.sharding import PartitionSpec as P

BF = jnp.bfloat16
F32 = jnp.float32
VM = pl.BlockSpec(memory_space=pltpu.VMEM)
SM = pl.BlockSpec(memory_space=pltpu.SMEM)
MIB = 1024 * 1024
CODE_ROWS = 16
PIECES = 2
STEP = 32
SENT = 64
TINY = pl.CostEstimate(flops=1000, bytes_accessed=1000, transcendentals=0)


def mm(a, b):
    return jnp.dot(a, b, preferred_element_type=F32)


def in_top():
    return lax.axis_index("sec") == 0


def owned(which_set):
    return lax.axis_index("tile") % 2 == which_set


def message_kernel(row_ref, col_ref, count_ref, ints_ref, strip_ref, out, second):
    second[...] = strip_ref[1:2]
    slots, size, n = out.shape
    half = size - CODE_ROWS
    start = pl.multiple_of(lax.axis_index("sec") * half, half)
    out[:, :half, :] = ints_ref[:, pl.ds(start, half), :]
    at_row = lax.broadcasted_iota(jnp.int32, (CODE_ROWS, n), 0)
    values = [row_ref[w] for w in range(slots)] + [col_ref[w] for w in range(slots)]
    codes = jnp.zeros((CODE_ROWS, n), F32)
    for k, value in enumerate(values + [count_ref[0]]):
        codes = jnp.where(at_row == k, value.astype(F32), codes)
    for w in range(slots):
        out[w, half:, :] = codes.astype(BF)


def place_waves(corners, live, own, probe_ref, own_here, own_there, marks, rolled, seen):
    n = probe_ref.shape[1]
    rows = lax.broadcasted_iota(jnp.int32, (n, n), 0)
    cols = lax.broadcasted_iota(jnp.int32, (n, n), 1)
    at_row = lax.broadcasted_iota(jnp.int32, (8, n), 0)
    top = in_top()
    for w, (r, c) in enumerate(corners):
        weight = jnp.where(w < live, 2, 0)
        signed = r if own else -r
        marks[w] = jnp.where(at_row == 0, signed, jnp.where(at_row == 1, c, weight))
        mine, left = (rows >= r) if own else (rows < r), cols >= c
        for part in range(2):
            plane = pltpu.roll(probe_ref[part].astype(F32), r, 0)
            rolled[w, part] = pltpu.roll(plane, c, 1).astype(BF)

            def choose(ref):
                plane = ref[part, 0].astype(F32)
                both = jnp.where(left, plane[:, :n], plane[:, n:])
                return jnp.where(mine, both, 0.0).astype(BF)

            here, there = choose(own_here), choose(own_there)

            @pl.when(top)
            def _():
                seen[w, 0, part] = here
                seen[w, 1, part] = there

            @pl.when(jnp.logical_not(top))
            def _():
                seen[w, 0, part] = there
                seen[w, 1, part] = here


def own_kernel(
    row_ref, col_ref, count_ref, phase_ref, probe_ref, own_here, own_there,
    near_left, near_right, far_left, far_right, marks, rolled, seen,
):
    n = probe_ref.shape[1]
    slots = rolled.shape[0]
    phase = jnp.broadcast_to(phase_ref[...], (8, n))
    turn = jnp.where(
        lax.broadcasted_iota(jnp.int32, (8, n), 0) == 0, jnp.cos(phase), jnp.sin(phase)
    )

    def exact(a, b):
        return jnp.dot(a, b, precision=lax.Precision.HIGHEST, preferred_element_type=F32)

    product = lax.broadcasted_iota(jnp.int32, (n, n), 0) * lax.broadcasted_iota(
        jnp.int32, (n, n), 1
    )
    angles = lax.rem(product, n).astype(F32) * (2.0 * math.pi / n)
    cosine, sine = jnp.cos(angles), jnp.sin(angles)
    by_cos = exact(turn, cosine)
    by_sin = exact(turn, sine)
    scale = 1.0 / n

    def circulant(row):
        return pltpu.roll(
            jnp.broadcast_to(row * scale, (n, n)), 0, 1, stride=1, stride_axis=0
        ).astype(BF)

    m_re, m_im = circulant(by_cos[0:1] + by_sin[1:2]), circulant(by_cos[1:2] - by_sin[0:1])
    t_re, t_im = circulant(by_cos[0:1] - by_sin[1:2]), circulant(by_cos[1:2] + by_sin[0:1])
    f_re, f_im = (cosine / math.sqrt(n)).astype(BF), (-sine / math.sqrt(n)).astype(BF)

    def fill(table, re, im, low):
        table[:n, :n] = re
        table[n:, n:] = re
        table[:n, n:] = -im if low else im
        table[n:, :n] = im if low else -im

    fill(near_left, m_re, m_im, True)
    fill(near_right, t_re, t_im, False)
    fill(far_left, f_re, f_im, True)
    fill(far_right, f_re, f_im, False)
    corners = [(row_ref[w], col_ref[w]) for w in range(slots)]
    place_waves(
        corners, count_ref[0], True, probe_ref, own_here, own_there, marks, rolled, seen
    )


def past_kernel(received, probe_ref, own_here, own_there, marks, rolled, seen):
    slots, n = rolled.shape[0], rolled.shape[2]
    height = received.shape[1] - CODE_ROWS
    codes = received[0, height:].astype(F32)
    at_row = lax.broadcasted_iota(jnp.int32, codes.shape, 0)

    def decode(k):
        return jnp.max(jnp.where(at_row == k, codes, 0.0)).astype(jnp.int32)

    corners = [(decode(w), decode(slots + w)) for w in range(slots)]
    place_waves(
        corners, decode(2 * slots), False, probe_ref, own_here, own_there, marks, rolled, seen
    )


class Waves:
    def __init__(self, which_set, placed, near, far, work):
        self.placed, self.near, self.far = placed, near, far
        self.field, self.inner, self.outer, self.last = work
        self.slots, _, self.n, _ = placed[1].shape
        self.own = owned(which_set)
        self.flip = jnp.where(self.own, 0, -1)
        self.marks = [self.pick(0, w) for w in range(self.slots)]
        cols = lax.broadcasted_iota(jnp.int32, (STEP, self.n), 1)
        self.left = [cols >= mark[1:2] for mark in self.marks]

    def pick(self, kind, *at):
        return jnp.where(self.own, self.placed[kind][at], self.placed[3 + kind][at])

    def rows(self):
        return [slice(at, at + STEP) for at in range(0, self.n, STEP)]

    def mine(self, w, at):
        index = lax.broadcasted_iota(jnp.int32, (STEP, self.n), 0) + at.start
        return (index ^ self.flip) >= self.marks[w][0:1]

    def window(self, w, layer, other, at):
        n = self.n
        mine, left = self.mine(w, at), self.left[w]
        planes = []
        for part in range(2):
            pieces = other[part]
            size = n // len(pieces)
            piece, first = pieces[at.start // size], at.start % size
            plane = piece[0, first : first + STEP, :].astype(F32)
            outside = jnp.where(left, plane[:, :n], plane[:, n:])
            inside = self.pick(2, w, layer, part, at).astype(F32)
            planes.append(jnp.where(mine, inside, outside))
        return planes

    def probe(self, w, at):
        return [self.pick(1, w, part, at).astype(F32) for part in range(2)]

    def pair(self, ref, w, at):
        return ref[w, 0, at, :].astype(F32), ref[w, 1, at, :].astype(F32)

    def put(self, w, at, re, im):
        n = self.n
        lower = slice(n + at.start, n + at.stop)
        self.field[at, w * n : (w + 1) * n] = re.astype(BF)
        self.field[lower, w * n : (w + 1) * n] = im.astype(BF)

    def got(self, w, at):
        n = self.n
        here = slice(w * n + at.start, w * n + at.stop)
        return self.outer[here, :n], self.outer[here, n:]

    def propagate(self, left, right):
        n = self.n
        for w in range(self.slots):
            product = mm(left[...], self.field[:, w * n : (w + 1) * n]).astype(BF)
            self.inner[w * n : (w + 1) * n, :n] = product[:n]
            self.inner[w * n : (w + 1) * n, n:] = product[n:]
        for w in range(self.slots):
            here = slice(w * n, (w + 1) * n)
            self.outer[here, :] = mm(self.inner[here, :], right[...])

    def enter(self, other, psi):
        for w in range(self.slots):
            for at in self.rows():
                t_re, t_im = self.window(w, 0, other, at)
                p_re, p_im = self.probe(w, at)
                self.put(w, at, t_re * p_re - t_im * p_im, t_re * p_im + t_im * p_re)
        self.propagate(*self.near)
        for w in range(self.slots):
            for at in self.rows():
                re, im = self.got(w, at)
                psi[w, 0, at, :] = re.astype(BF)
                psi[w, 1, at, :] = im.astype(BF)

    def leave(self, other, psi, own_int, int_here, int_there):
        for w in range(self.slots):
            for at in self.rows():
                t_re, t_im = self.window(w, 1, other, at)
                self.last[w, 0, at, :] = t_re.astype(BF)
                self.last[w, 1, at, :] = t_im.astype(BF)
                p_re, p_im = self.pair(psi, w, at)
                self.put(w, at, t_re * p_re - t_im * p_im, t_re * p_im + t_im * p_re)
        self.propagate(*self.far)
        half = self.n // 2
        top = in_top()
        for w in range(self.slots):
            weight = self.marks[w][2:3].astype(F32)
            for at in self.rows():
                re, im = self.got(w, at)
                part = slice(at.start % half, at.start % half + STEP)
                is_here = top == (at.start < half)
                received = jnp.where(
                    is_here, int_here[w, part, :].astype(F32), int_there[w, part, :].astype(F32)
                )
                measured = jnp.where(self.own, own_int[w, at, :].astype(F32), received)
                factor = weight * (re * re + im * im - measured)
                self.put(w, at, factor * re, factor * im)
        self.propagate(self.far[1], self.far[0])

    def reach_first(self):
        for w in range(self.slots):
            for at in self.rows():
                t_re, t_im = self.pair(self.last, w, at)
                y_re, y_im = (part.astype(BF).astype(F32) for part in self.got(w, at))
                self.put(w, at, t_re * y_re + t_im * y_im, t_re * y_im - t_im * y_re)
        self.propagate(self.near[1], self.near[0])

    def gradient(self, entering, base, out, final=None, sems=None):
        n = self.n
        copies = []
        for at in self.rows():
            sums = [0.0] * 4
            if base is not None:
                sums = [base[part, 0, at, c : c + n] for part in range(2) for c in (0, n)]
            for w in range(self.slots):
                mine, left = self.mine(w, at), self.left[w]
                a_re, a_im = entering(w, at)
                y_re, y_im = (part.astype(BF).astype(F32) for part in self.got(w, at))
                values = (a_re * y_re + a_im * y_im, a_re * y_im - a_im * y_re)
                for part, value in enumerate(values):
                    value = jnp.where(mine, value, 0.0)
                    first = jnp.where(left, value, 0.0)
                    sums[2 * part] = sums[2 * part] + first
                    sums[2 * part + 1] = sums[2 * part + 1] + (value - first)
            for part in range(2):
                out[part, 0, at, :n] = sums[2 * part]
                out[part, 0, at, n:] = sums[2 * part + 1]
            if final is not None and at.stop % SENT == 0:
                done = slice(at.stop - SENT, at.stop)
                copy = pltpu.make_async_copy(
                    out.at[:, :, done, :], final.at[:, :, done, :], sems.at[len(copies)]
                )
                copy.start()
                copies.append(copy)
        for copy in copies:
            copy.wait()


def facing_kernel(here_re, here_im, there_re, *refs):
    there_im, refs = refs[:PIECES], refs[PIECES:]
    (
        own_int, int_here, int_there, nl, nr, fl, fr, m0, r0, s0, m1, r1, s1,
        out, field, inner, outer, last, psi,
    ) = refs
    placed = (m0, r0, s0, m1, r1, s1)
    waves = Waves(0, placed, (nl, nr), (fl, fr), (field, inner, outer, last))
    ints = (own_int, int_here, int_there)
    here = [[here_re.at[0]], [here_im.at[0]]]
    there = [[there_re.at[0]], [piece.at[0] for piece in there_im]]
    top = in_top()

    @pl.when(top)
    def _():
        waves.enter(here, psi)
        waves.leave(there, psi, *ints)
        waves.reach_first()
        waves.gradient(waves.probe, None, out)

    @pl.when(jnp.logical_not(top))
    def _():
        waves.enter(there, psi)
        waves.leave(here, psi, *ints)
        waves.gradient(lambda w, at: waves.pair(psi, w, at), None, out)


def entering_kernel(
    here_re, here_im, nl, nr, m0, r0, s0, m1, r1, s1, psi, field, inner, outer, last
):
    @pl.when(in_top())
    def _():
        placed = (m0, r0, s0, m1, r1, s1)
        waves = Waves(1, placed, (nl, nr), None, (field, inner, outer, last))
        waves.enter([[here_re.at[0]], [here_im.at[0]]], psi)


def opposite_kernel(
    here_re, here_im, there_re, there_im, own_int, int_here, int_there, nl, nr, fl, fr,
    m0, r0, s0, m1, r1, s1, entered, base, out, field, inner, outer, last, psi, total, sems,
):
    placed = (m0, r0, s0, m1, r1, s1)
    waves = Waves(1, placed, (nl, nr), (fl, fr), (field, inner, outer, last))
    ints = (own_int, int_here, int_there)
    here, there = [[here_re.at[0]], [here_im.at[0]]], [[there_re.at[0]], [there_im.at[0]]]
    top = in_top()

    @pl.when(top)
    def _():
        waves.leave(there, entered, *ints)
        waves.reach_first()
        waves.gradient(waves.probe, base, total, out, sems)

    @pl.when(jnp.logical_not(top))
    def _():
        waves.enter(there, psi)
        waves.leave(here, psi, *ints)
        waves.gradient(lambda w, at: waves.pair(psi, w, at), base, total, out, sems)


def kernel_call(kernel, name, out_shape, in_specs, scratch_shapes=(), out_spec=VM):
    many = isinstance(out_shape, tuple)
    return pl.pallas_call(
        kernel,
        out_shape=out_shape,
        in_specs=in_specs,
        out_specs=(VM,) * len(out_shape) if many else out_spec,
        scratch_shapes=scratch_shapes,
        compiler_params=pltpu.CompilerParams(vmem_limit_bytes=16 * MIB),
        cost_estimate=TINY,
        name=name,
    )


def on_device(obj, probe, phases, intensities, pos_row, pos_col, counts):
    n = probe.shape[1]
    slots = pos_row.shape[0]
    tiles = lax.axis_size("tile")
    half = intensities.shape[1] // lax.axis_size("sec")
    after = lax.optimization_barrier

    def swap(value):
        return lax.ppermute(value, "sec", [(0, 1), (1, 0)])

    def send(value, pairs):
        inside = [(a, b) for a, b in pairs if 0 <= min(a, b) and max(a, b) < tiles]
        return lax.ppermute(value, "tile", inside)

    onward = [(i, i + 1) for i in range(tiles)]
    paired = [(i, i ^ 1) for i in range(tiles)]
    relayed = [(i, i - 2 if i % 2 else i + 2) for i in range(tiles)]

    sideways = [(b, a) for a, b in relayed]
    facing_re = send(obj[0:1], paired)
    crossed = send(obj[1:2], sideways)
    opposite_im = send(crossed, paired)
    own_there = swap(obj)
    positions = (pos_row, pos_col, counts)
    cut = (1, *obj.shape[1:])
    message, second = kernel_call(
        message_kernel,
        "message",
        (
            jax.ShapeDtypeStruct((slots, half + CODE_ROWS, n), BF),
            jax.ShapeDtypeStruct(cut, BF),
        ),
        [SM] * 3 + [VM] * 2,
    )(*positions, intensities, obj)
    facing_im = send(second, paired)
    int_here = send(message, onward)
    opposite_re = send(facing_re, relayed)
    phases, _ = after((phases, facing_re))

    double = jax.ShapeDtypeStruct((2 * n, 2 * n), BF)
    wave_shapes = (
        jax.ShapeDtypeStruct((slots, 8, n), jnp.int32),
        jax.ShapeDtypeStruct((slots, 2, n, n), BF),
        jax.ShapeDtypeStruct((slots, 2, 2, n, n), BF),
    )
    nl, nr, fl, fr, *own_waves = kernel_call(
        own_kernel, "own", (double,) * 4 + wave_shapes, [SM] * 3 + [VM] * 4
    )(*positions, phases[None], probe, obj, own_there)
    facing_im, nl = after((facing_im, nl))
    int_here, _ = after((int_here, facing_im))
    int_there = swap(int_here)
    past_waves = kernel_call(past_kernel, "past", wave_shapes, [VM] * 4)(
        int_here, probe, obj, own_there
    )
    placed = (*own_waves, *past_waves)

    work = [
        pltpu.VMEM((2 * n, slots * n), BF),
        pltpu.VMEM((slots * n, 2 * n), BF),
        pltpu.VMEM((slots * n, 2 * n), F32),
    ]
    def pieces(value):
        step = value.shape[2] // PIECES
        return [swap(value[:, :, at : at + step]) for at in range(0, value.shape[2], step)]

    pair = pltpu.VMEM((slots, 2, n, n), BF)
    work.append(pair)
    ints = (intensities, int_here, int_there)
    grad_shape = jax.ShapeDtypeStruct(obj.shape, F32)
    partial = kernel_call(
        facing_kernel, "facing", grad_shape, [VM] * (16 + PIECES), work + [pair]
    )(facing_re, facing_im, swap(facing_re), *pieces(facing_im), *ints, nl, nr, fl, fr, *placed)
    opposite_re_there = swap(opposite_re)
    opposite_im, partial = after((opposite_im, partial))
    opposite = (opposite_re, opposite_im)
    opposite_there = (opposite_re_there, swap(opposite_im))
    entered = kernel_call(
        entering_kernel, "entering", jax.ShapeDtypeStruct((slots, 2, n, n), BF), [VM] * 10, work
    )(*opposite, nl, nr, *placed)
    return kernel_call(
        opposite_kernel,
        "opposite",
        grad_shape,
        [VM] * 19,
        work + [pair, pltpu.VMEM(obj.shape, F32), pltpu.SemaphoreType.DMA((n // SENT,))],
        out_spec=pl.BlockSpec(memory_space=pltpu.HBM),
    )(*opposite, *opposite_there, *ints, nl, nr, fl, fr, *placed, entered, partial)


def solution(mesh):
    placed = (
        P(None, "sec", "tile", None),
        P(),
        P(),
        P("tile", None, None),
        P("tile"),
        P("tile"),
        P("tile"),
    )
    return jax.shard_map(
        on_device,
        mesh=mesh,
        in_specs=placed,
        out_specs=P(None, "sec", "tile", None),
        check_vma=False,
    )
```

```python
import math

import jax
import jax.numpy as jnp
import numpy as np
from jax import lax
from jax.experimental import pallas as pl
from jax.experimental.pallas import tpu as pltpu
from jax.sharding import PartitionSpec as P

BF = jnp.bfloat16
F32 = jnp.float32
VM = pl.BlockSpec(memory_space=pltpu.VMEM)
SM = pl.BlockSpec(memory_space=pltpu.SMEM)
MIB = 1024 * 1024
CODE_ROWS = 16
PIECES = 2
STEP = 32
SENT = 64
TINY = pl.CostEstimate(flops=1000, bytes_accessed=1000, transcendentals=0)


def mm(a, b):
    return jnp.dot(a, b, preferred_element_type=F32)


def in_top():
    return lax.axis_index("sec") == 0


def owned(which_set):
    return lax.axis_index("tile") % 2 == which_set


def message_kernel(row_ref, col_ref, count_ref, ints_ref, strip_ref, out, second):
    second[...] = strip_ref[1:2]
    slots, size, n = out.shape
    half = size - CODE_ROWS
    start = pl.multiple_of(lax.axis_index("sec") * half, half)
    out[:, :half, :] = ints_ref[:, pl.ds(start, half), :]
    at_row = lax.broadcasted_iota(jnp.int32, (CODE_ROWS, n), 0)
    values = [row_ref[w] for w in range(slots)] + [col_ref[w] for w in range(slots)]
    codes = jnp.zeros((CODE_ROWS, n), F32)
    for k, value in enumerate(values + [count_ref[0]]):
        codes = jnp.where(at_row == k, value.astype(F32), codes)
    for w in range(slots):
        out[w, half:, :] = codes.astype(BF)


def place_waves(corners, live, own, probe_ref, own_here, own_there, marks, rolled, seen):
    n = probe_ref.shape[1]
    rows = lax.broadcasted_iota(jnp.int32, (n, n), 0)
    cols = lax.broadcasted_iota(jnp.int32, (n, n), 1)
    at_row = lax.broadcasted_iota(jnp.int32, (8, n), 0)
    top = in_top()
    for w, (r, c) in enumerate(corners):
        weight = jnp.where(w < live, 2, 0)
        signed = r if own else -r
        marks[w] = jnp.where(at_row == 0, signed, jnp.where(at_row == 1, c, weight))
        mine, left = (rows >= r) if own else (rows < r), cols >= c
        for part in range(2):
            plane = pltpu.roll(probe_ref[part].astype(F32), r, 0)
            rolled[w, part] = pltpu.roll(plane, c, 1).astype(BF)

            def choose(ref):
                plane = ref[part, 0].astype(F32)
                both = jnp.where(left, plane[:, :n], plane[:, n:])
                return jnp.where(mine, both, 0.0).astype(BF)

            here, there = choose(own_here), choose(own_there)

            @pl.when(top)
            def _():
                seen[w, 0, part] = here
                seen[w, 1, part] = there

            @pl.when(jnp.logical_not(top))
            def _():
                seen[w, 0, part] = there
                seen[w, 1, part] = here


def own_kernel(
    row_ref, col_ref, count_ref, phase_ref, probe_ref, own_here, own_there,
    near_left, near_right, far_left, far_right, marks, rolled, seen,
):
    n = probe_ref.shape[1]
    slots = rolled.shape[0]
    phase = jnp.broadcast_to(phase_ref[...], (8, n))
    turn = jnp.where(
        lax.broadcasted_iota(jnp.int32, (8, n), 0) == 0, jnp.cos(phase), jnp.sin(phase)
    )

    def exact(a, b):
        return jnp.dot(a, b, precision=lax.Precision.HIGHEST, preferred_element_type=F32)

    product = lax.broadcasted_iota(jnp.int32, (n, n), 0) * lax.broadcasted_iota(
        jnp.int32, (n, n), 1
    )
    angles = lax.rem(product, n).astype(F32) * (2.0 * math.pi / n)
    cosine, sine = jnp.cos(angles), jnp.sin(angles)
    by_cos = exact(turn, cosine)
    by_sin = exact(turn, sine)
    scale = 1.0 / n

    def circulant(row):
        return pltpu.roll(
            jnp.broadcast_to(row * scale, (n, n)), 0, 1, stride=1, stride_axis=0
        ).astype(BF)

    m_re, m_im = circulant(by_cos[0:1] + by_sin[1:2]), circulant(by_cos[1:2] - by_sin[0:1])
    t_re, t_im = circulant(by_cos[0:1] - by_sin[1:2]), circulant(by_cos[1:2] + by_sin[0:1])
    f_re, f_im = (cosine / math.sqrt(n)).astype(BF), (-sine / math.sqrt(n)).astype(BF)

    def fill(table, re, im, low):
        table[:n, :n] = re
        table[n:, n:] = re
        table[:n, n:] = -im if low else im
        table[n:, :n] = im if low else -im

    fill(near_left, m_re, m_im, True)
    fill(near_right, t_re, t_im, False)
    fill(far_left, f_re, f_im, True)
    fill(far_right, f_re, f_im, False)
    corners = [(row_ref[w], col_ref[w]) for w in range(slots)]
    place_waves(
        corners, count_ref[0], True, probe_ref, own_here, own_there, marks, rolled, seen
    )


def past_kernel(received, probe_ref, own_here, own_there, marks, rolled, seen):
    slots, n = rolled.shape[0], rolled.shape[2]
    height = received.shape[1] - CODE_ROWS
    codes = received[0, height:].astype(F32)
    at_row = lax.broadcasted_iota(jnp.int32, codes.shape, 0)

    def decode(k):
        return jnp.max(jnp.where(at_row == k, codes, 0.0)).astype(jnp.int32)

    corners = [(decode(w), decode(slots + w)) for w in range(slots)]
    place_waves(
        corners, decode(2 * slots), False, probe_ref, own_here, own_there, marks, rolled, seen
    )


class Waves:
    def __init__(self, which_set, placed, near, far, work):
        self.placed, self.near, self.far = placed, near, far
        self.field, self.inner, self.outer, self.last = work
        self.slots, _, self.n, _ = placed[1].shape
        self.own = owned(which_set)
        self.flip = jnp.where(self.own, 0, -1)
        self.marks = [self.pick(0, w) for w in range(self.slots)]
        cols = lax.broadcasted_iota(jnp.int32, (STEP, self.n), 1)
        self.left = [cols >= mark[1:2] for mark in self.marks]

    def pick(self, kind, *at):
        return jnp.where(self.own, self.placed[kind][at], self.placed[3 + kind][at])

    def rows(self):
        return [slice(at, at + STEP) for at in range(0, self.n, STEP)]

    def mine(self, w, at):
        index = lax.broadcasted_iota(jnp.int32, (STEP, self.n), 0) + at.start
        return (index ^ self.flip) >= self.marks[w][0:1]

    def window(self, w, layer, other, at):
        n = self.n
        mine, left = self.mine(w, at), self.left[w]
        planes = []
        for part in range(2):
            pieces = other[part]
            size = n // len(pieces)
            piece, first = pieces[at.start // size], at.start % size
            plane = piece[0, first : first + STEP, :].astype(F32)
            outside = jnp.where(left, plane[:, :n], plane[:, n:])
            inside = self.pick(2, w, layer, part, at).astype(F32)
            planes.append(jnp.where(mine, inside, outside))
        return planes

    def probe(self, w, at):
        return [self.pick(1, w, part, at).astype(F32) for part in range(2)]

    def pair(self, ref, w, at):
        return ref[w, 0, at, :].astype(F32), ref[w, 1, at, :].astype(F32)

    def put(self, w, at, re, im):
        n = self.n
        lower = slice(n + at.start, n + at.stop)
        self.field[at, w * n : (w + 1) * n] = re.astype(BF)
        self.field[lower, w * n : (w + 1) * n] = im.astype(BF)

    def got(self, w, at):
        n = self.n
        here = slice(w * n + at.start, w * n + at.stop)
        return self.outer[here, :n], self.outer[here, n:]

    def right_rows(self, at):
        n = self.n
        here = [slice(w * n + at.start, w * n + at.stop) for w in range(self.slots)]
        product = mm(
            jnp.concatenate([self.inner[rows, :] for rows in here], axis=0), self.pending[...]
        )
        size = at.stop - at.start
        for w, rows in enumerate(here):
            self.outer[rows, :] = product[w * size : (w + 1) * size]

    def propagate(self, left, right, defer=False):
        n = self.n
        for w in range(self.slots):
            product = mm(left[...], self.field[:, w * n : (w + 1) * n]).astype(BF)
            self.inner[w * n : (w + 1) * n, :n] = product[:n]
            self.inner[w * n : (w + 1) * n, n:] = product[n:]
        self.pending = right if defer else None
        for w in range(0 if defer else self.slots):
            here = slice(w * n, (w + 1) * n)
            self.outer[here, :] = mm(self.inner[here, :], right[...])

    def enter(self, other, psi):
        for w in range(self.slots):
            for at in self.rows():
                t_re, t_im = self.window(w, 0, other, at)
                p_re, p_im = self.probe(w, at)
                self.put(w, at, t_re * p_re - t_im * p_im, t_re * p_im + t_im * p_re)
        self.propagate(*self.near)
        for w in range(self.slots):
            for at in self.rows():
                re, im = self.got(w, at)
                psi[w, 0, at, :] = re.astype(BF)
                psi[w, 1, at, :] = im.astype(BF)

    def leave(self, other, psi, own_int, int_here, int_there, defer=False):
        for w in range(self.slots):
            for at in self.rows():
                t_re, t_im = self.window(w, 1, other, at)
                self.last[w, 0, at, :] = t_re.astype(BF)
                self.last[w, 1, at, :] = t_im.astype(BF)
                p_re, p_im = self.pair(psi, w, at)
                self.put(w, at, t_re * p_re - t_im * p_im, t_re * p_im + t_im * p_re)
        self.propagate(*self.far)
        half = self.n // 2
        top = in_top()
        for w in range(self.slots):
            weight = self.marks[w][2:3].astype(F32)
            for at in self.rows():
                re, im = self.got(w, at)
                part = slice(at.start % half, at.start % half + STEP)
                is_here = top == (at.start < half)
                received = jnp.where(
                    is_here, int_here[w, part, :].astype(F32), int_there[w, part, :].astype(F32)
                )
                measured = jnp.where(self.own, own_int[w, at, :].astype(F32), received)
                factor = weight * (re * re + im * im - measured)
                self.put(w, at, factor * re, factor * im)
        self.propagate(self.far[1], self.far[0], defer)

    def reach_first(self, defer=False):
        for w in range(self.slots):
            for at in self.rows():
                t_re, t_im = self.pair(self.last, w, at)
                y_re, y_im = (part.astype(BF).astype(F32) for part in self.got(w, at))
                self.put(w, at, t_re * y_re + t_im * y_im, t_re * y_im - t_im * y_re)
        self.propagate(self.near[1], self.near[0], defer)

    def gradient(self, entering, base, out, final=None, sems=None):
        n = self.n
        copies = []
        for at in self.rows():
            if self.pending is not None and at.start % SENT == 0:
                self.right_rows(slice(at.start, at.start + SENT))
            sums = [0.0] * 4
            if base is not None:
                sums = [base[part, 0, at, c : c + n] for part in range(2) for c in (0, n)]
            for w in range(self.slots):
                mine, left = self.mine(w, at), self.left[w]
                a_re, a_im = entering(w, at)
                y_re, y_im = (part.astype(BF).astype(F32) for part in self.got(w, at))
                values = (a_re * y_re + a_im * y_im, a_re * y_im - a_im * y_re)
                for part, value in enumerate(values):
                    value = jnp.where(mine, value, 0.0)
                    first = jnp.where(left, value, 0.0)
                    sums[2 * part] = sums[2 * part] + first
                    sums[2 * part + 1] = sums[2 * part + 1] + (value - first)
            for part in range(2):
                out[part, 0, at, :n] = sums[2 * part]
                out[part, 0, at, n:] = sums[2 * part + 1]
            if final is not None and at.stop % SENT == 0:
                done = slice(at.stop - SENT, at.stop)
                copy = pltpu.make_async_copy(
                    out.at[:, :, done, :], final.at[:, :, done, :], sems.at[len(copies)]
                )
                copy.start()
                copies.append(copy)
        for copy in copies:
            copy.wait()


def facing_kernel(here_re, here_im, there_re, *refs):
    there_im, refs = refs[:PIECES], refs[PIECES:]
    (
        own_int, int_here, int_there, nl, nr, fl, fr, m0, r0, s0, m1, r1, s1,
        out, field, inner, outer, last, psi,
    ) = refs
    placed = (m0, r0, s0, m1, r1, s1)
    waves = Waves(0, placed, (nl, nr), (fl, fr), (field, inner, outer, last))
    ints = (own_int, int_here, int_there)
    here = [[here_re.at[0]], [here_im.at[0]]]
    there = [[there_re.at[0]], [piece.at[0] for piece in there_im]]
    top = in_top()

    @pl.when(top)
    def _():
        waves.enter(here, psi)
        waves.leave(there, psi, *ints)
        waves.reach_first()
        waves.gradient(waves.probe, None, out)

    @pl.when(jnp.logical_not(top))
    def _():
        waves.enter(there, psi)
        waves.leave(here, psi, *ints)
        waves.gradient(lambda w, at: waves.pair(psi, w, at), None, out)


def entering_kernel(
    here_re, here_im, nl, nr, m0, r0, s0, m1, r1, s1, psi, field, inner, outer, last
):
    @pl.when(in_top())
    def _():
        placed = (m0, r0, s0, m1, r1, s1)
        waves = Waves(1, placed, (nl, nr), None, (field, inner, outer, last))
        waves.enter([[here_re.at[0]], [here_im.at[0]]], psi)


def opposite_kernel(
    here_re, here_im, there_re, there_im, own_int, int_here, int_there, nl, nr, fl, fr,
    m0, r0, s0, m1, r1, s1, entered, base, out, field, inner, outer, last, psi, total, sems,
):
    placed = (m0, r0, s0, m1, r1, s1)
    waves = Waves(1, placed, (nl, nr), (fl, fr), (field, inner, outer, last))
    ints = (own_int, int_here, int_there)
    here, there = [[here_re.at[0]], [here_im.at[0]]], [[there_re.at[0]], [there_im.at[0]]]
    top = in_top()

    @pl.when(top)
    def _():
        waves.leave(there, entered, *ints)
        waves.reach_first(defer=True)
        waves.gradient(waves.probe, base, total, out, sems)

    @pl.when(jnp.logical_not(top))
    def _():
        waves.enter(there, psi)
        waves.leave(here, psi, *ints, defer=True)
        waves.gradient(lambda w, at: waves.pair(psi, w, at), base, total, out, sems)


def kernel_call(kernel, name, out_shape, in_specs, scratch_shapes=(), out_spec=VM):
    many = isinstance(out_shape, tuple)
    return pl.pallas_call(
        kernel,
        out_shape=out_shape,
        in_specs=in_specs,
        out_specs=(VM,) * len(out_shape) if many else out_spec,
        scratch_shapes=scratch_shapes,
        compiler_params=pltpu.CompilerParams(vmem_limit_bytes=16 * MIB),
        cost_estimate=TINY,
        name=name,
    )


def on_device(obj, probe, phases, intensities, pos_row, pos_col, counts):
    n = probe.shape[1]
    slots = pos_row.shape[0]
    tiles = lax.axis_size("tile")
    half = intensities.shape[1] // lax.axis_size("sec")
    after = lax.optimization_barrier

    def swap(value):
        return lax.ppermute(value, "sec", [(0, 1), (1, 0)])

    def send(value, pairs):
        inside = [(a, b) for a, b in pairs if 0 <= min(a, b) and max(a, b) < tiles]
        return lax.ppermute(value, "tile", inside)

    onward = [(i, i + 1) for i in range(tiles)]
    paired = [(i, i ^ 1) for i in range(tiles)]
    relayed = [(i, i - 2 if i % 2 else i + 2) for i in range(tiles)]

    sideways = [(b, a) for a, b in relayed]
    facing_re = send(obj[0:1], paired)
    crossed = send(obj[1:2], sideways)
    opposite_im = send(crossed, paired)
    own_there = swap(obj)
    positions = (pos_row, pos_col, counts)
    cut = (1, *obj.shape[1:])
    message, second = kernel_call(
        message_kernel,
        "message",
        (
            jax.ShapeDtypeStruct((slots, half + CODE_ROWS, n), BF),
            jax.ShapeDtypeStruct(cut, BF),
        ),
        [SM] * 3 + [VM] * 2,
    )(*positions, intensities, obj)
    facing_im = send(second, paired)
    int_here = send(message, onward)
    opposite_re = send(facing_re, relayed)
    phases, _ = after((phases, facing_re))

    double = jax.ShapeDtypeStruct((2 * n, 2 * n), BF)
    wave_shapes = (
        jax.ShapeDtypeStruct((slots, 8, n), jnp.int32),
        jax.ShapeDtypeStruct((slots, 2, n, n), BF),
        jax.ShapeDtypeStruct((slots, 2, 2, n, n), BF),
    )
    nl, nr, fl, fr, *own_waves = kernel_call(
        own_kernel, "own", (double,) * 4 + wave_shapes, [SM] * 3 + [VM] * 4
    )(*positions, phases[None], probe, obj, own_there)
    facing_im, nl = after((facing_im, nl))
    int_here, _ = after((int_here, facing_im))
    int_there = swap(int_here)
    past_waves = kernel_call(past_kernel, "past", wave_shapes, [VM] * 4)(
        int_here, probe, obj, own_there
    )
    placed = (*own_waves, *past_waves)

    work = [
        pltpu.VMEM((2 * n, slots * n), BF),
        pltpu.VMEM((slots * n, 2 * n), BF),
        pltpu.VMEM((slots * n, 2 * n), F32),
    ]
    def pieces(value):
        step = value.shape[2] // PIECES
        return [swap(value[:, :, at : at + step]) for at in range(0, value.shape[2], step)]

    pair = pltpu.VMEM((slots, 2, n, n), BF)
    work.append(pair)
    ints = (intensities, int_here, int_there)
    grad_shape = jax.ShapeDtypeStruct(obj.shape, F32)
    partial = kernel_call(
        facing_kernel, "facing", grad_shape, [VM] * (16 + PIECES), work + [pair]
    )(facing_re, facing_im, swap(facing_re), *pieces(facing_im), *ints, nl, nr, fl, fr, *placed)
    opposite_re_there = swap(opposite_re)
    opposite_im, partial = after((opposite_im, partial))
    opposite = (opposite_re, opposite_im)
    opposite_there = (opposite_re_there, swap(opposite_im))
    entered = kernel_call(
        entering_kernel, "entering", jax.ShapeDtypeStruct((slots, 2, n, n), BF), [VM] * 10, work
    )(*opposite, nl, nr, *placed)
    return kernel_call(
        opposite_kernel,
        "opposite",
        grad_shape,
        [VM] * 19,
        work + [pair, pltpu.VMEM(obj.shape, F32), pltpu.SemaphoreType.DMA((n // SENT,))],
        out_spec=pl.BlockSpec(memory_space=pltpu.HBM),
    )(*opposite, *opposite_there, *ints, nl, nr, fl, fr, *placed, entered, partial)


def solution(mesh):
    placed = (
        P(None, "sec", "tile", None),
        P(),
        P(),
        P("tile", None, None),
        P("tile"),
        P("tile"),
        P("tile"),
    )
    return jax.shard_map(
        on_device,
        mesh=mesh,
        in_specs=placed,
        out_specs=P(None, "sec", "tile", None),
        check_vma=False,
    )
```
